32 devices in a mesh: blk: 8 (over z, core), feat: 4 (over y, x).
Axes of the slice: x: 2, y: 2, z: 4, core: 2. Of those that a mesh axis runs over, the one named last changes fastest.
Arguments:
- grads: float32 [4096, 8192], P('blk', 'feat'), may hold values from -3000 to 3000
Outputs:
- cosine: float32 [4096, 4096], P('blk', 'feat')
The draws below stay inside these ranges and needn't reach their ends.
All inputs are finite; a program needn't handle non-finite values.
Results may differ from the reference program's by a relative error of at most 0.000053.
Values sent between devices are 32-bit elements; how exact they have to be, the bound alone decides.
A program may use at most 128 MiB of HBM per device.

```python
import math
import jax
import jax.numpy as jnp
from jax import lax

FEAT = 8192
ROWS = 4096


def draw_grads(key, part):
    keys = jax.random.split(key, 5)
    noise = jax.random.normal(keys[0], (ROWS, FEAT), jnp.float32)
    common = 0.6
    coeff = jax.random.normal(keys[1], (ROWS, 1), jnp.float32)
    direction = jax.random.normal(keys[2], (1, FEAT), jnp.float32)
    row_scale = jnp.exp(jax.random.uniform(keys[3], (ROWS, 1), jnp.float32, 0.0, math.log(10.0)))
    col_scale = jnp.exp(jax.random.uniform(keys[4], (1, FEAT), jnp.float32, 0.0, math.log(10.0)))
    values = row_scale * col_scale * (noise + common * coeff * direction)
    return jnp.clip(values, -3000.0, 3000.0)


def setup_inputs(seed: int = 0) -> dict:
    key_list = jax.random.split(jax.random.key(seed), 2)
    grads = draw_grads(jax.random.fold_in(key_list[1], 71), 0)
    return {"grads": grads}


def reference(grads):
    gram = lax.dot_general(grads, grads, (((1,), (1,)), ((), ())), precision=lax.Precision.HIGHEST, preferred_element_type=jnp.float32)
    squares = lax.optimization_barrier(jnp.sum(grads * grads, axis=1))
    inverse = 1.0 / jnp.sqrt(squares + 1e-06)
    return gram * inverse[:, None] * inverse[None, :]
```

```python
import jax
import jax.numpy as jnp
from jax import lax
from jax.sharding import PartitionSpec as P


def passed_along(value, axis, steps):
    count = lax.axis_size(axis)
    pairs = [(source, (source + steps) % count) for source in range(count)]
    return lax.ppermute(value, axis, pairs)


def tile_of(left, right):
    return lax.dot_general(
        left,
        right,
        (((1,), (1,)), ((), ())),
        precision=lax.Precision.HIGHEST,
        preferred_element_type=jnp.float32,
    )


def place(partial_value, piece, column):
    offset = column * piece.shape[1]
    return lax.dynamic_update_slice(partial_value, piece, (jnp.int32(0), offset))


def local(grads):
    rows = grads.shape[0]
    blocks = lax.axis_size("blk")
    mine = lax.axis_index("blk")
    partial_value = jnp.zeros((rows, blocks * rows), jnp.float32)
    partial_value = place(partial_value, tile_of(grads, grads), mine)
    half = blocks // 2
    held = grads
    for step in range(1, half + 1):
        held = passed_along(held, "blk", 1)
        piece = tile_of(grads, held)
        partial_value = place(partial_value, piece, (mine - step) % blocks)
        if step < half:
            back = passed_along(piece.T, "blk", -step)
            partial_value = place(partial_value, back, (mine + step) % blocks)
    gram = lax.psum_scatter(partial_value, "feat", scatter_dimension=1, tiled=True)
    squares = lax.psum(jnp.sum(grads * grads, axis=1), "feat")
    every = lax.all_gather(squares, "blk", axis=0, tiled=True)
    width = gram.shape[1]
    column_sq = lax.dynamic_slice_in_dim(every, lax.axis_index("feat") * width, width)
    row_inverse = 1.0 / jnp.sqrt(squares + 1e-06)
    column_inverse = 1.0 / jnp.sqrt(column_sq + 1e-06)
    return gram * row_inverse[:, None] * column_inverse[None, :]


BOTH = ("blk", "feat")


def product(left, right):
    return lax.dot_general(
        left,
        right,
        (((1,), (1,)), ((), ())),
        precision=lax.Precision.HIGH,
        preferred_element_type=jnp.float32,
    )


def where_is(z, core, f):
    return (2 * z + core) * 4 + f


def mirrored(core, value):
    return value if core == 0 else 3 - value


def along(value, moves):
    pairs = [
        (2 * mirrored(core, a) + core, 2 * mirrored(core, b) + core)
        for core in range(2)
        for a, b in moves
    ]
    return lax.ppermute(value, "blk", pairs)


def other_core(value):
    count = lax.axis_size("blk")
    return lax.ppermute(value, "blk", [(i, i ^ 1) for i in range(count)])


def partner(value, bit):
    return lax.ppermute(value, "feat", [(f, f ^ bit) for f in range(4)])


def onto(value, targets, bit_order):
    first, second = bit_order
    pairs = [
        (where_is(z, c, f), where_is(z, c, f ^ first))
        for z, t in targets.items()
        for c in range(2)
        for f in range(4)
        if (f ^ t) & first
    ]
    value = value + lax.ppermute(value, BOTH, pairs)
    pairs = [
        (where_is(z, c, t ^ second), where_is(z, c, t))
        for z, t in targets.items()
        for c in range(2)
    ]
    return value + lax.ppermute(value, BOTH, pairs)


def rows_to_target(block, core, targets):
    rows = block.shape[0] // 2
    halves = block.reshape(2, rows, block.shape[1])
    mine = lax.dynamic_index_in_dim(halves, core, 0, False)
    give = lax.dynamic_index_in_dim(halves, 1 - core, 0, False)
    mine = mine + other_core(give)
    width = mine.shape[1] // 2
    return jnp.concatenate(
        [onto(mine[:, :width], targets, (1, 2)), onto(mine[:, width:], targets, (2, 1))],
        axis=1,
    )


PIECES = {
    (0, 0): (2, 0), (1, 0): (3, 1), (2, 0): (2, 1), (3, 0): (3, 0),
    (0, 1): (3, 0), (1, 1): (2, 1), (2, 1): (2, 0), (3, 1): (3, 1),
}


def meeting(near_or_far, core, g, k, half):
    a, b = PIECES[g, k]
    source = where_is(mirrored(core, 2), core, mirrored(core, g))
    za, zb = mirrored(core, a), mirrored(core, b)
    if near_or_far == "near":
        return (source, where_is(za, half, zb))
    return (source, where_is(zb, g // 2, za))


def scattered(blocks, row_half, g):
    rows = blocks[2, 0].shape[0] // 2
    width = blocks[2, 0].shape[1] // 2

    def piece(gg, k):
        a, b = PIECES[gg, k]
        h = gg // 2
        return blocks[a, b][row_half * rows : (row_half + 1) * rows, h * width : (h + 1) * width]

    gy, gx = g // 2, g % 2
    if row_half == 0:
        stack = jnp.stack(
            [jnp.stack([jnp.stack([piece(2 * y + x, k) for k in range(2)]) for x in range(2)]) for y in range(2)]
        )
        first, second, bits = gy, gx, (2, 1)
    else:
        stack = jnp.stack(
            [jnp.stack([jnp.stack([piece(2 * y + x, k) for k in range(2)]) for y in range(2)]) for x in range(2)]
        )
        first, second, bits = gx, gy, (1, 2)
    got = partner(lax.dynamic_index_in_dim(stack, 1 - first, 0, False), bits[0])
    kept = lax.dynamic_index_in_dim(stack, first, 0, False) + got
    got = partner(lax.dynamic_index_in_dim(kept, 1 - second, 0, False), bits[1])
    return lax.dynamic_index_in_dim(kept, second, 0, False) + got


def met(grads):
    rows, depth = grads.shape
    mine, f = lax.axis_index("blk"), lax.axis_index("feat")
    core, z = mine % 2, mine // 2
    position = jnp.where(core == 0, z, 3 - z)
    g = jnp.where(core == 0, f, 3 - f)

    total = lax.axis_size("blk") * rows
    squares = jnp.sum(grads * grads, axis=1)
    every = lax.dynamic_update_slice_in_dim(
        jnp.zeros((total,), jnp.float32), squares, mine * rows, 0
    )
    every = lax.psum(every, BOTH)

    half = depth // 2
    kept = lax.dynamic_slice_in_dim(grads, core * half, half, 1)
    got = other_core(lax.dynamic_slice_in_dim(grads, (1 - core) * half, half, 1))
    own = jnp.where(
        core == 0, jnp.concatenate([kept, got], 0), jnp.concatenate([got, kept], 0)
    )

    one = along(own, [(0, 1), (1, 2)])
    own_later, one = lax.optimization_barrier((own, one))
    zero = along(one, [(1, 2)])
    three = along(own_later, [(3, 2)])

    diagonal = product(own, own)
    diagonal = rows_to_target(diagonal, core, {z_: z_ for z_ in range(4)})
    b21 = product(own, one)
    b23 = product(own, three)
    inner = jnp.where(position == 1, b21, b23)
    inner = rows_to_target(inner, core, {1: 0, 2: 3})

    blocks = {
        (2, 1): b21,
        (3, 1): product(three, one),
        (2, 0): product(own, zero),
        (3, 0): product(three, zero),
    }
    upper = scattered(blocks, 0, g)
    lower = scattered(blocks, 1, g)

    cross = None
    for k in range(2):
        far = jnp.concatenate([upper[k].T, lower[k].T], axis=1)
        pairs = [meeting("far", c, gg, k, 0) for c in range(2) for gg in range(4)]
        far = lax.ppermute(far, BOTH, pairs)
        cross = far if cross is None else cross + far
    near = []
    for k in range(2):
        parts = []
        for h, value in enumerate((upper, lower)):
            pairs = [meeting("near", c, gg, k, h) for c in range(2) for gg in range(4)]
            parts.append(lax.ppermute(value[k], BOTH, pairs))
        near.append(parts[0] + parts[1])
    straight = (z - f) * (z - f) == 4
    left = jnp.where(straight, near[0], near[1])
    right = jnp.where(straight, near[1], near[0])
    cross = cross + jnp.concatenate([left, right], axis=1)

    width = inner.shape[1] // 2
    column_halves = jnp.stack([inner[:, :width].T, inner[:, width:].T])
    ends = [((1, 0), (0, 1)), ((2, 3), (3, 2))]
    same = lax.ppermute(
        lax.dynamic_index_in_dim(column_halves, core, 0, False),
        BOTH,
        [(where_is(a, c, b), where_is(p, c, q)) for (a, b), (p, q) in ends for c in range(2)],
    )
    swapped = lax.ppermute(
        lax.dynamic_index_in_dim(column_halves, 1 - core, 0, False),
        BOTH,
        [(where_is(a, c, b), where_is(p, 1 - c, q)) for (a, b), (p, q) in ends for c in range(2)],
    )
    outer = jnp.concatenate(
        [jnp.where(core == 0, same, swapped), jnp.where(core == 0, swapped, same)], axis=1
    )

    is_inner = ((z == 1) & (f == 0)) | ((z == 2) & (f == 3))
    is_outer = ((z == 0) & (f == 1)) | ((z == 3) & (f == 2))
    gram = jnp.where(z == f, diagonal, jnp.where(is_inner, inner, jnp.where(is_outer, outer, cross)))

    columns = gram.shape[1]
    row_sq = lax.dynamic_slice_in_dim(every, mine * rows, rows)
    column_sq = lax.dynamic_slice_in_dim(every, f * columns, columns)
    row_inverse = 1.0 / jnp.sqrt(row_sq + 1e-06)
    column_inverse = 1.0 / jnp.sqrt(column_sq + 1e-06)
    return gram * row_inverse[:, None] * column_inverse[None, :]


def solution(mesh):
    placed = (P("blk", "feat"),)
    body = met if (mesh.shape["blk"], mesh.shape["feat"]) == (8, 4) else local
    return jax.shard_map(
        body, mesh=mesh, in_specs=placed, out_specs=P("blk", "feat"), check_vma=False
    )
```

```python
import jax
import jax.numpy as jnp
from jax import lax
from jax.sharding import PartitionSpec as P


def passed_along(value, axis, steps):
    count = lax.axis_size(axis)
    pairs = [(source, (source + steps) % count) for source in range(count)]
    return lax.ppermute(value, axis, pairs)


def tile_of(left, right):
    return lax.dot_general(
        left,
        right,
        (((1,), (1,)), ((), ())),
        precision=lax.Precision.HIGHEST,
        preferred_element_type=jnp.float32,
    )


def place(partial_value, piece, column):
    offset = column * piece.shape[1]
    return lax.dynamic_update_slice(partial_value, piece, (jnp.int32(0), offset))


def local(grads):
    rows = grads.shape[0]
    blocks = lax.axis_size("blk")
    mine = lax.axis_index("blk")
    partial_value = jnp.zeros((rows, blocks * rows), jnp.float32)
    partial_value = place(partial_value, tile_of(grads, grads), mine)
    half = blocks // 2
    held = grads
    for step in range(1, half + 1):
        held = passed_along(held, "blk", 1)
        piece = tile_of(grads, held)
        partial_value = place(partial_value, piece, (mine - step) % blocks)
        if step < half:
            back = passed_along(piece.T, "blk", -step)
            partial_value = place(partial_value, back, (mine + step) % blocks)
    gram = lax.psum_scatter(partial_value, "feat", scatter_dimension=1, tiled=True)
    squares = lax.psum(jnp.sum(grads * grads, axis=1), "feat")
    every = lax.all_gather(squares, "blk", axis=0, tiled=True)
    width = gram.shape[1]
    column_sq = lax.dynamic_slice_in_dim(every, lax.axis_index("feat") * width, width)
    row_inverse = 1.0 / jnp.sqrt(squares + 1e-06)
    column_inverse = 1.0 / jnp.sqrt(column_sq + 1e-06)
    return gram * row_inverse[:, None] * column_inverse[None, :]


BOTH = ("blk", "feat")


def product(left, right):
    return lax.dot_general(
        left,
        right,
        (((1,), (1,)), ((), ())),
        precision=lax.Precision.HIGH,
        preferred_element_type=jnp.float32,
    )


def where_is(z, core, f):
    return (2 * z + core) * 4 + f


def mirrored(core, value):
    return value if core == 0 else 3 - value


def along(value, moves):
    pairs = [
        (2 * mirrored(core, a) + core, 2 * mirrored(core, b) + core)
        for core in range(2)
        for a, b in moves
    ]
    return lax.ppermute(value, "blk", pairs)


def other_core(value):
    count = lax.axis_size("blk")
    return lax.ppermute(value, "blk", [(i, i ^ 1) for i in range(count)])


def partner(value, bit):
    return lax.ppermute(value, "feat", [(f, f ^ bit) for f in range(4)])


def first_sum(value, targets, bit):
    pairs = [
        (where_is(z, c, f), where_is(z, c, f ^ bit))
        for z, t in targets.items()
        for c in range(2)
        for f in range(4)
        if (f ^ t) & bit
    ]
    return value + lax.ppermute(value, BOTH, pairs)


def second_sum(value, targets, bit):
    pairs = [
        (where_is(z, c, t ^ bit), where_is(z, c, t))
        for z, t in targets.items()
        for c in range(2)
    ]
    return value + lax.ppermute(value, BOTH, pairs)


def own_rows(block, core):
    rows = block.shape[0] // 2
    halves = block.reshape(2, rows, block.shape[1])
    mine = lax.dynamic_index_in_dim(halves, core, 0, False)
    give = lax.dynamic_index_in_dim(halves, 1 - core, 0, False)
    mine = mine + other_core(give)
    width = mine.shape[1] // 2
    return mine[:, :width], mine[:, width:]


def first_sums(pair, targets):
    return first_sum(pair[0], targets, 1), first_sum(pair[1], targets, 2)


def second_sums(pair, targets):
    return jnp.concatenate(
        [second_sum(pair[0], targets, 2), second_sum(pair[1], targets, 1)], axis=1
    )


PIECES = {
    (0, 0): (2, 0), (1, 0): (3, 1), (2, 0): (2, 1), (3, 0): (3, 0),
    (0, 1): (3, 0), (1, 1): (2, 1), (2, 1): (2, 0), (3, 1): (3, 1),
}


def meeting(near_or_far, core, g, k, half):
    a, b = PIECES[g, k]
    source = where_is(mirrored(core, 2), core, mirrored(core, g))
    za, zb = mirrored(core, a), mirrored(core, b)
    if near_or_far == "near":
        return (source, where_is(za, half, zb))
    return (source, where_is(zb, g // 2, za))


def scattered(blocks, row_half, g):
    rows = blocks[2, 0].shape[0] // 2
    width = blocks[2, 0].shape[1] // 2

    def piece(gg, k):
        a, b = PIECES[gg, k]
        h = gg // 2
        return blocks[a, b][row_half * rows : (row_half + 1) * rows, h * width : (h + 1) * width]

    gy, gx = g // 2, g % 2
    if row_half == 0:
        stack = jnp.stack(
            [jnp.stack([jnp.stack([piece(2 * y + x, k) for k in range(2)]) for x in range(2)]) for y in range(2)]
        )
        first, bits = gy, (2, 1)
    else:
        stack = jnp.stack(
            [jnp.stack([jnp.stack([piece(2 * y + x, k) for k in range(2)]) for y in range(2)]) for x in range(2)]
        )
        first, bits = gx, (1, 2)
    got = partner(lax.dynamic_index_in_dim(stack, 1 - first, 0, False), bits[0])
    return lax.dynamic_index_in_dim(stack, first, 0, False) + got


def scattered_on(kept, row_half, g):
    second, bit = (g % 2, 1) if row_half == 0 else (g // 2, 2)
    got = partner(lax.dynamic_index_in_dim(kept, 1 - second, 0, False), bit)
    return lax.dynamic_index_in_dim(kept, second, 0, False) + got


def met(grads):
    rows, depth = grads.shape
    mine, f = lax.axis_index("blk"), lax.axis_index("feat")
    core, z = mine % 2, mine // 2
    position = jnp.where(core == 0, z, 3 - z)
    g = jnp.where(core == 0, f, 3 - f)

    total = lax.axis_size("blk") * rows
    squares = jnp.sum(grads * grads, axis=1)
    every = lax.dynamic_update_slice_in_dim(
        jnp.zeros((total,), jnp.float32), squares, mine * rows, 0
    )

    half = depth // 2
    kept = lax.dynamic_slice_in_dim(grads, core * half, half, 1)
    got = other_core(lax.dynamic_slice_in_dim(grads, (1 - core) * half, half, 1))
    own = jnp.where(
        core == 0, jnp.concatenate([kept, got], 0), jnp.concatenate([got, kept], 0)
    )

    one = along(own, [(0, 1), (1, 2)])
    every = lax.psum(every, BOTH)
    on_diagonal = {z_: z_ for z_ in range(4)}
    diagonal = first_sums(own_rows(product(own, own), core), on_diagonal)
    own, one, every, diagonal = lax.optimization_barrier((own, one, every, diagonal))
    zero = along(one, [(1, 2)])
    three = along(own, [(3, 2)])
    b21 = product(own, one)
    diagonal = second_sums(diagonal, on_diagonal)
    zero, three, b21, diagonal = lax.optimization_barrier((zero, three, b21, diagonal))

    blocks = {
        (2, 1): b21,
        (3, 1): product(three, one),
        (2, 0): product(own, zero),
        (3, 0): product(three, zero),
    }
    upper = scattered(blocks, 0, g)
    lower = scattered(blocks, 1, g)
    blocks, three = lax.optimization_barrier((blocks, three))
    b23 = product(own, three)
    inner_to = {1: 0, 2: 3}
    inner = own_rows(jnp.where(position == 1, blocks[2, 1], b23), core)
    upper, lower, inner = lax.optimization_barrier((upper, lower, inner))
    upper = scattered_on(upper, 0, g)
    lower = scattered_on(lower, 1, g)
    inner = first_sums(inner, inner_to)
    upper, lower, inner = lax.optimization_barrier((upper, lower, inner))
    inner = second_sums(inner, inner_to)

    cross = None
    for k in range(2):
        far = jnp.concatenate([upper[k].T, lower[k].T], axis=1)
        pairs = [meeting("far", c, gg, k, 0) for c in range(2) for gg in range(4)]
        far = lax.ppermute(far, BOTH, pairs)
        cross = far if cross is None else cross + far
    near = []
    for k in range(2):
        parts = []
        for h, value in enumerate((upper, lower)):
            pairs = [meeting("near", c, gg, k, h) for c in range(2) for gg in range(4)]
            parts.append(lax.ppermute(value[k], BOTH, pairs))
        near.append(parts[0] + parts[1])
    straight = (z - f) * (z - f) == 4
    left = jnp.where(straight, near[0], near[1])
    right = jnp.where(straight, near[1], near[0])
    cross = cross + jnp.concatenate([left, right], axis=1)

    width = inner.shape[1] // 2
    column_halves = jnp.stack([inner[:, :width].T, inner[:, width:].T])
    ends = [((1, 0), (0, 1)), ((2, 3), (3, 2))]
    same = lax.ppermute(
        lax.dynamic_index_in_dim(column_halves, core, 0, False),
        BOTH,
        [(where_is(a, c, b), where_is(p, c, q)) for (a, b), (p, q) in ends for c in range(2)],
    )
    swapped = lax.ppermute(
        lax.dynamic_index_in_dim(column_halves, 1 - core, 0, False),
        BOTH,
        [(where_is(a, c, b), where_is(p, 1 - c, q)) for (a, b), (p, q) in ends for c in range(2)],
    )
    outer = jnp.concatenate(
        [jnp.where(core == 0, same, swapped), jnp.where(core == 0, swapped, same)], axis=1
    )

    is_inner = ((z == 1) & (f == 0)) | ((z == 2) & (f == 3))
    is_outer = ((z == 0) & (f == 1)) | ((z == 3) & (f == 2))
    gram = jnp.where(z == f, diagonal, jnp.where(is_inner, inner, jnp.where(is_outer, outer, cross)))

    columns = gram.shape[1]
    row_sq = lax.dynamic_slice_in_dim(every, mine * rows, rows)
    column_sq = lax.dynamic_slice_in_dim(every, f * columns, columns)
    row_inverse = 1.0 / jnp.sqrt(row_sq + 1e-06)
    column_inverse = 1.0 / jnp.sqrt(column_sq + 1e-06)
    return gram * row_inverse[:, None] * column_inverse[None, :]


def solution(mesh):
    placed = (P("blk", "feat"),)
    body = met if (mesh.shape["blk"], mesh.shape["feat"]) == (8, 4) else local
    return jax.shard_map(
        body, mesh=mesh, in_specs=placed, out_specs=P("blk", "feat"), check_vma=False
    )
```

```python
import jax
import jax.numpy as jnp
from jax import lax
from jax.sharding import PartitionSpec as P


def passed_along(value, axis, steps):
    count = lax.axis_size(axis)
    pairs = [(source, (source + steps) % count) for source in range(count)]
    return lax.ppermute(value, axis, pairs)


def tile_of(left, right):
    return lax.dot_general(
        left,
        right,
        (((1,), (1,)), ((), ())),
        precision=lax.Precision.HIGH,
        preferred_element_type=jnp.float32,
    )


def place(partial_value, piece, column):
    offset = column * piece.shape[1]
    return lax.dynamic_update_slice(partial_value, piece, (jnp.int32(0), offset))


def local(grads):
    rows = grads.shape[0]
    blocks = lax.axis_size("blk")
    mine = lax.axis_index("blk")
    half = blocks // 2
    held = passed_along(grads, "blk", 1)
    squares = lax.psum(jnp.sum(grads * grads, axis=1), "feat")
    every = lax.all_gather(squares, "blk", axis=0, tiled=True)
    piece = tile_of(grads, grads)
    held, squares, every, piece = lax.optimization_barrier((held, squares, every, piece))
    partial_value = jnp.zeros((rows, blocks * rows), jnp.float32)
    partial_value = place(partial_value, piece, mine)
    for step in range(1, half + 1):
        piece = tile_of(grads, held)
        partial_value = place(partial_value, piece, (mine - step) % blocks)
        if step < half:
            coming = passed_along(held, "blk", 1)
            back = passed_along(piece.T, "blk", -step)
            held, back = lax.optimization_barrier((coming, back))
            partial_value = place(partial_value, back, (mine + step) % blocks)
    gram = lax.psum_scatter(partial_value, "feat", scatter_dimension=1, tiled=True)
    width = gram.shape[1]
    column_sq = lax.dynamic_slice_in_dim(every, lax.axis_index("feat") * width, width)
    row_inverse = 1.0 / jnp.sqrt(squares + 1e-06)
    column_inverse = 1.0 / jnp.sqrt(column_sq + 1e-06)
    return gram * row_inverse[:, None] * column_inverse[None, :]


def solution(mesh):
    placed = (P("blk", "feat"),)
    return jax.shard_map(
        local, mesh=mesh, in_specs=placed, out_specs=P("blk", "feat"), check_vma=False
    )
```

```python
import jax
import jax.numpy as jnp
from jax import lax
from jax.sharding import PartitionSpec as P


def passed_along(value, axis, steps):
    count = lax.axis_size(axis)
    pairs = [(source, (source + steps) % count) for source in range(count)]
    return lax.ppermute(value, axis, pairs)


def tile_of(left, right):
    return lax.dot_general(
        left,
        right,
        (((1,), (1,)), ((), ())),
        precision=lax.Precision.HIGH,
        preferred_element_type=jnp.float32,
    )


def summed_at(piece, shift):
    blocks, feats = lax.axis_size("blk"), lax.axis_size("feat")
    per = blocks // feats
    bits = [1 << i for i in range(feats.bit_length() - 1)]
    half = piece.shape[1] // 2
    sums = []
    for value, order in ((piece[:, :half], bits), (piece[:, half:], bits[::-1])):
        done = 0
        for bit in order:
            pairs = []
            for block in range(blocks):
                target = (block + shift) % blocks // per
                pairs += [
                    (block * feats + f, block * feats + (f ^ bit))
                    for f in range(feats)
                    if (f ^ target) & bit and not (f ^ target) & done
                ]
            value = value + lax.ppermute(value, ("blk", "feat"), pairs)
            done |= bit
        sums.append(value)
    return jnp.concatenate(sums, axis=1)


def local(grads):
    blocks, feats = lax.axis_size("blk"), lax.axis_size("feat")
    mine, column = lax.axis_index("blk"), lax.axis_index("feat")
    half = blocks // 2
    sums = {}
    held = passed_along(grads, "blk", 1)
    squares = lax.psum(jnp.sum(grads * grads, axis=1), "feat")
    every = lax.all_gather(squares, "blk", axis=0, tiled=True)
    piece = tile_of(grads, grads)
    held, squares, every, piece = lax.optimization_barrier((held, squares, every, piece))
    waiting = (0, piece)
    for step in range(1, half + 1):
        piece = tile_of(grads, held)
        shift = (blocks - step) % blocks
        if step < half:
            coming = passed_along(held, "blk", 1)
            back = passed_along(piece.T, "blk", -step)
            sums[waiting[0]] = summed_at(waiting[1], waiting[0])
            sums[shift] = summed_at(piece, shift)
            held, back, sums[waiting[0]], sums[shift] = lax.optimization_barrier(
                (coming, back, sums[waiting[0]], sums[shift])
            )
            waiting = (step, back)
        else:
            sums[waiting[0]] = summed_at(waiting[1], waiting[0])
            sums[shift] = summed_at(piece, shift)
    per = blocks // feats
    columns = []
    for q in range(per):
        wanted = (column * per + q - mine) % blocks
        chosen = sums[0]
        for shift in range(1, blocks):
            chosen = jnp.where(wanted == shift, sums[shift], chosen)
        columns.append(chosen)
    gram = jnp.concatenate(columns, axis=1)
    width = gram.shape[1]
    column_sq = lax.dynamic_slice_in_dim(every, column * width, width)
    row_inverse = 1.0 / jnp.sqrt(squares + 1e-06)
    column_inverse = 1.0 / jnp.sqrt(column_sq + 1e-06)
    return gram * row_inverse[:, None] * column_inverse[None, :]


def solution(mesh):
    placed = (P("blk", "feat"),)
    return jax.shard_map(
        local, mesh=mesh, in_specs=placed, out_specs=P("blk", "feat"), check_vma=False
    )
```

```python
import jax
import jax.numpy as jnp
from jax import lax
from jax.sharding import PartitionSpec as P


def position_of(block, count):
    return (block // 2) * (1 - block % 2) + (count - 1 - block // 2) * (block % 2)


def ring_order(count):
    return sorted(range(count), key=lambda block: position_of(block, count))


def passed_along(value, axis, steps):
    count = lax.axis_size(axis)
    order = ring_order(count)
    pairs = [(order[p], order[(p + steps) % count]) for p in range(count)]
    return lax.ppermute(value, axis, pairs)


def tile_of(left, right):
    return lax.dot_general(
        left,
        right,
        (((1,), (1,)), ((), ())),
        precision=lax.Precision.HIGH,
        preferred_element_type=jnp.float32,
    )


def summed_at(piece, shift):
    blocks, feats = lax.axis_size("blk"), lax.axis_size("feat")
    per = blocks // feats
    bits = [1 << i for i in range(feats.bit_length() - 1)]
    half = piece.shape[1] // 2
    order_of = ring_order(blocks)
    sums = []
    for value, order in ((piece[:, :half], bits), (piece[:, half:], bits[::-1])):
        done = 0
        for bit in order:
            pairs = []
            for block in range(blocks):
                target = order_of[(position_of(block, blocks) + shift) % blocks] // per
                pairs += [
                    (block * feats + f, block * feats + (f ^ bit))
                    for f in range(feats)
                    if (f ^ target) & bit and not (f ^ target) & done
                ]
            value = value + lax.ppermute(value, ("blk", "feat"), pairs)
            done |= bit
        sums.append(value)
    return jnp.concatenate(sums, axis=1)


def local(grads):
    blocks, feats = lax.axis_size("blk"), lax.axis_size("feat")
    mine, column = lax.axis_index("blk"), lax.axis_index("feat")
    half = blocks // 2
    sums = {}
    held = passed_along(grads, "blk", 1)
    squares = lax.psum(jnp.sum(grads * grads, axis=1), "feat")
    every = lax.all_gather(squares, "blk", axis=0, tiled=True)
    piece = tile_of(grads, grads)
    held, squares, every, piece = lax.optimization_barrier((held, squares, every, piece))
    waiting = (0, piece)
    for step in range(1, half + 1):
        piece = tile_of(grads, held)
        shift = (blocks - step) % blocks
        if step < half:
            coming = passed_along(held, "blk", 1)
            back = passed_along(piece.T, "blk", -step)
            sums[waiting[0]] = summed_at(waiting[1], waiting[0])
            sums[shift] = summed_at(piece, shift)
            if step == half - 1:
                sums[step] = summed_at(back, step)
                coming, sums = lax.optimization_barrier((coming, sums))
                held = coming
                continue
            held, back, sums[waiting[0]], sums[shift] = lax.optimization_barrier(
                (coming, back, sums[waiting[0]], sums[shift])
            )
            waiting = (step, back)
        else:
            sums[shift] = summed_at(piece, shift)
    per = blocks // feats
    columns = []
    for q in range(per):
        wanted = (
            position_of(column * per + q, blocks) - position_of(mine, blocks)
        ) % blocks
        chosen = sums[0]
        for shift in range(1, blocks):
            chosen = jnp.where(wanted == shift, sums[shift], chosen)
        columns.append(chosen)
    gram = jnp.concatenate(columns, axis=1)
    width = gram.shape[1]
    column_sq = lax.dynamic_slice_in_dim(every, column * width, width)
    row_inverse = 1.0 / jnp.sqrt(squares + 1e-06)
    column_inverse = 1.0 / jnp.sqrt(column_sq + 1e-06)
    return gram * row_inverse[:, None] * column_inverse[None, :]


def solution(mesh):
    placed = (P("blk", "feat"),)
    return jax.shard_map(
        local, mesh=mesh, in_specs=placed, out_specs=P("blk", "feat"), check_vma=False
    )
```

```python
import jax
import jax.numpy as jnp
from jax import lax
from jax.sharding import PartitionSpec as P


def position_of(block, count):
    return (block // 2) * (1 - block % 2) + (count - 1 - block // 2) * (block % 2)


def ring_order(count):
    return sorted(range(count), key=lambda block: position_of(block, count))


def passed_along(value, axis, steps):
    count = lax.axis_size(axis)
    order = ring_order(count)
    pairs = [(order[p], order[(p + steps) % count]) for p in range(count)]
    return lax.ppermute(value, axis, pairs)


def tile_of(left, right):
    return lax.dot_general(
        left,
        right,
        (((1,), (1,)), ((), ())),
        precision=lax.Precision.HIGH,
        preferred_element_type=jnp.float32,
    )


def summed_at(piece, shift):
    blocks, feats = lax.axis_size("blk"), lax.axis_size("feat")
    per = blocks // feats
    bits = [1 << i for i in range(feats.bit_length() - 1)]
    half = piece.shape[1] // 2
    order_of = ring_order(blocks)
    sums = []
    for value, order in ((piece[:, :half], bits), (piece[:, half:], bits[::-1])):
        done = 0
        for bit in order:
            pairs = []
            for block in range(blocks):
                target = order_of[(position_of(block, blocks) + shift) % blocks] // per
                pairs += [
                    (block * feats + f, block * feats + (f ^ bit))
                    for f in range(feats)
                    if (f ^ target) & bit and not (f ^ target) & done
                ]
            value = value + lax.ppermute(value, ("blk", "feat"), pairs)
            done |= bit
        sums.append(value)
    return jnp.concatenate(sums, axis=1)


def local(grads):
    blocks, feats = lax.axis_size("blk"), lax.axis_size("feat")
    mine, column = lax.axis_index("blk"), lax.axis_index("feat")
    half = blocks // 2
    sums = {}
    held = passed_along(grads, "blk", 1)
    squares = lax.psum(jnp.sum(grads * grads, axis=1), "feat")
    every = lax.all_gather(squares, "blk", axis=0, tiled=True)
    grads, held, squares, every = lax.optimization_barrier((grads, held, squares, every))
    waiting = (0, tile_of(grads, grads))
    for step in range(1, half + 1):
        piece = tile_of(grads, held)
        shift = (blocks - step) % blocks
        if step < half:
            coming = passed_along(held, "blk", 1)
            back = passed_along(piece.T, "blk", -step)
            sums[waiting[0]] = summed_at(waiting[1], waiting[0])
            sums[shift] = summed_at(piece, shift)
            if step == half - 1:
                held, sums = lax.optimization_barrier((coming, sums))
                sums[step] = summed_at(back, step)
                continue
            held, back, sums[waiting[0]], sums[shift] = lax.optimization_barrier(
                (coming, back, sums[waiting[0]], sums[shift])
            )
            waiting = (step, back)
        else:
            sums[shift] = summed_at(piece, shift)
    per = blocks // feats
    columns = []
    for q in range(per):
        wanted = (
            position_of(column * per + q, blocks) - position_of(mine, blocks)
        ) % blocks
        chosen = sums[0]
        for shift in range(1, blocks):
            chosen = jnp.where(wanted == shift, sums[shift], chosen)
        columns.append(chosen)
    gram = jnp.concatenate(columns, axis=1)
    width = gram.shape[1]
    column_sq = lax.dynamic_slice_in_dim(every, column * width, width)
    row_inverse = 1.0 / jnp.sqrt(squares + 1e-06)
    column_inverse = 1.0 / jnp.sqrt(column_sq + 1e-06)
    return gram * row_inverse[:, None] * column_inverse[None, :]


def solution(mesh):
    placed = (P("blk", "feat"),)
    return jax.shard_map(
        local, mesh=mesh, in_specs=placed, out_specs=P("blk", "feat"), check_vma=False
    )
```
